32 devices in a mesh: rows: 4 (over x, core), vec: 8 (over z, y).
Axes of the slice: x: 2, y: 2, z: 4, core: 2. Of those that a mesh axis runs over, the one named last changes fastest.
Arguments:
- eigen_rows: float32 [2048, 1024], P('rows', 'vec'), may hold values from -6 to 6
- panels: float32 [3, 2048, 256], P(None, ('rows', 'vec')), may hold values from -0.25 to 0.25
Outputs:
- transformed: float32 [2048, 1024], P('rows', 'vec')
The draws below stay inside these ranges and needn't reach their ends.
All inputs are finite; a program needn't handle non-finite values.
Results may differ from the reference program's by a relative error of at most 0.00017.
Values sent between devices are 32-bit elements; how exact they have to be, the bound alone decides.
A program may use at most 192 MiB of HBM per device.

```python
import jax
import jax.numpy as jnp
from jax import lax

REFLECTORS = 256
BLOCK_ROWS = 512
SLOTS = 3
ROWS = 2048
VECTORS = 1024


def block_scale(stream_key, shape, cuts, smallest, largest):
    gain, own = 1.0, jax.random.fold_in(stream_key, 6)
    for dim, blocks in cuts:
        steps = jnp.exp(jax.random.uniform(jax.random.fold_in(own, dim), (blocks,), jnp.float32, smallest / len(cuts), largest / len(cuts)))
        gain = gain * jnp.repeat(steps, shape[dim] // blocks).reshape([-1 if axis == dim else 1 for axis in range(len(shape))])
    return gain


def scatter_about(key, extent, scale, most, shards=(), held_as=jnp.bfloat16):
    array = jax.random.normal(key, extent, jnp.float32) * scale
    if len(shards) > 0:
        array = block_scale(key, extent, shards, -0.22, 0.18) * array
    return jnp.clip(array, min=-most, max=most).astype(held_as)


def setup_inputs(seed: int = 0) -> dict:
    streams_of = jax.random.split(jax.random.key(seed), 3)
    return {
        "eigen_rows": scatter_about(streams_of[0], (ROWS, VECTORS), 1.0, 6.0, ((0, 4), (1, 8)), jnp.float32),
        "panels": scatter_about(streams_of[1], (SLOTS, ROWS, REFLECTORS), BLOCK_ROWS ** -0.5, 0.25, ((1, 32),), jnp.float32),
    }


def reflect(panel_rows, values):
    block_len = panel_rows.shape[-2]
    width = panel_rows.shape[-1]
    shifted = panel_rows + jnp.eye(block_len, width, dtype=panel_rows.dtype)
    inner_products = jnp.einsum('...br,...bs->...rs', shifted, shifted, precision=lax.Precision.HIGHEST)
    triangle = jnp.triu(inner_products, 1) + 0.5 * inner_products * jnp.eye(width, dtype=panel_rows.dtype)
    projected = jnp.einsum('...br,...bc->...rc', shifted, values, precision=lax.Precision.HIGHEST)
    solved = jax.scipy.linalg.solve_triangular(triangle, projected, lower=False)
    return values - jnp.einsum('...br,...rc->...bc', shifted, solved, precision=lax.Precision.HIGHEST)

def reference(eigen_rows, panels):
    block_len = 2 * REFLECTORS
    columns = eigen_rows.shape[1]
    values = eigen_rows
    for sweep_set in range(SLOTS):
        offset = sweep_set % 2 * REFLECTORS
        pieces = (ROWS - 2 * offset) // block_len
        interior = values[offset:offset + pieces * block_len]
        panel_part = panels[sweep_set][offset:offset + pieces * block_len]
        applied = lax.map(lambda operands: reflect(operands[0], operands[1]), (panel_part.reshape(pieces, block_len, REFLECTORS), interior.reshape(pieces, block_len, columns)))
        applied = applied.reshape(pieces * block_len, columns)
        values = jnp.concatenate([values[:offset], applied, values[offset + pieces * block_len:]], axis=0)
    return values
```

```python
import functools

import jax
import jax.numpy as jnp
from jax import lax
from jax.experimental import pallas as pl
from jax.experimental.pallas import tpu as pltpu
from jax.sharding import PartitionSpec as P

MESH = pl.DeviceIdType.MESH
BASE = 8
F32, BF16 = jnp.float32, jnp.bfloat16


def split(a):
    high = a.astype(BF16)
    return high, (a - high.astype(F32)).astype(BF16)


def mm(a, b):
    ah, al = a
    bh, bl = b
    n = bh.shape[1]
    if n % 256:
        both = jnp.concatenate([bh, bl], axis=1)
        left = jnp.concatenate([ah, al], axis=1)
        out = jnp.dot(
            left, jnp.concatenate([both, both], axis=0), preferred_element_type=F32
        )
        return out[:, :n] + out[:, n:]
    dot = functools.partial(jnp.dot, preferred_element_type=F32)
    return dot(ah, bh) + (dot(ah, bl) + dot(al, bh))


def eye_of(rows, cols):
    r = lax.broadcasted_iota(jnp.int32, (rows, cols), 0)
    c = lax.broadcasted_iota(jnp.int32, (rows, cols), 1)
    return jnp.where(r == c, 1.0, 0.0).astype(F32)


def invert_all(grams):
    width = grams[0].shape[0]
    half = width // 2
    r = lax.broadcasted_iota(jnp.int32, (half, half), 0)
    c = lax.broadcasted_iota(jnp.int32, (half, half), 1)
    eye = jnp.where(r == c, 1.0, 0.0).astype(F32)
    parts, corners, scales = [], [], []
    for g in grams:
        d_rows = []
        d_cols = []
        for i in range(2):
            tile = g[i * half : (i + 1) * half, i * half : (i + 1) * half]
            diag = jnp.where(r == c, 0.5 * tile, 0.0)
            d_rows.append(1.0 / jnp.sum(diag, axis=0, keepdims=True))
            d_cols.append(1.0 / jnp.sum(diag, axis=1, keepdims=True))
            parts.append(jnp.where(c > r, tile * d_rows[i], 0.0))
        corners.append(g[:half, half:] * d_rows[1])
        scales.append(d_cols)
    small = [jnp.where(r // BASE == c // BASE, m, 0.0) for m in parts]
    pairs = [split(m) for m in small]
    powers = [mm(p, p) for p in pairs]
    inv = [eye - m for m in small]
    span = 2
    while span < BASE:
        pairs = [split(p) for p in powers]
        inv = [i + mm(split(i), p) for i, p in zip(inv, pairs)]
        span *= 2
        if span < BASE:
            powers = [mm(p, p) for p in pairs]
        else:
            break
    span = BASE
    while span < half:
        mask = jnp.logical_and(r // (2 * span) == c // (2 * span), r // span != c // span)
        cross = [split(jnp.where(mask, m, 0.0)) for m in parts]
        pairs = [split(i) for i in inv]
        mid = [mm(x, p) for x, p in zip(cross, pairs)]
        inv = [i - mm(p, split(m)) for i, p, m in zip(inv, pairs, mid)]
        span *= 2
    pairs = [split(i) for i in inv]
    mids = [mm(split(corners[k]), pairs[2 * k + 1]) for k in range(len(grams))]
    tops = [-mm(pairs[2 * k], split(mids[k])) for k in range(len(grams))]
    out = []
    for k in range(len(grams)):
        upper = jnp.concatenate([inv[2 * k], tops[k]], axis=1) * scales[k][0]
        lower = jnp.concatenate([jnp.zeros_like(tops[k]), inv[2 * k + 1]], axis=1) * scales[k][1]
        out.append(jnp.concatenate([upper, lower], axis=0))
    return out


def kernel(n, ng, z_ref, p_ref, out_ref, ybuf, gsend, grecv, wsend, wrecv,
           local_sem, send_sem, recv_sem, gs_sem, gr_sem, ws_sem, wr_sem):
    sets, shard, width = p_ref.shape
    steps = n // 2
    hw = width // 2
    g = lax.axis_index("rows")
    me = lax.axis_index("vec")
    odd = me % 2
    pos = (1 - odd) * (me // 2) + odd * (n - 1 - me // 2)

    def index_of(q):
        q = (q + 2 * n) % n
        first = 1 - (2 * q) // n
        return first * (2 * q) + (1 - first) * (2 * (n - 1 - q) + 1)

    sides = (index_of(pos + 1), index_of(pos - 1))
    has_up = g < ng - 1
    has_down = g > 0

    def slot(s, q, t, way):
        rows = pl.ds(pl.multiple_of(index_of(q) * shard, shard), shard)
        if t < steps - 1:
            return ybuf.at[s, rows, :]
        return ybuf.at[s, rows, pl.ds(way * hw, hw)]

    def sent(s, t, way):
        sign = 1 - 2 * way
        ref = slot(s, pos - sign * t, t, way)
        src = p_ref.at[s] if t == 0 and steps > 1 else ref
        return pltpu.make_async_remote_copy(
            src_ref=src, dst_ref=ref,
            send_sem=send_sem.at[s, way, t], recv_sem=recv_sem.at[s, way, t],
            device_id={"vec": sides[way]}, device_id_type=MESH)

    def arrived(s, t, way):
        sign = 1 - 2 * way
        ref = slot(s, pos - sign * (t + 1), t, way)
        return pltpu.make_async_remote_copy(
            src_ref=ref, dst_ref=ref,
            send_sem=send_sem.at[s, way, t], recv_sem=recv_sem.at[s, way, t],
            device_id={"vec": sides[way]}, device_id_type=MESH)

    def rim(src, dst, s_sem, r_sem, i):
        return pltpu.make_async_remote_copy(
            src_ref=src.at[i], dst_ref=dst.at[1 - i],
            send_sem=s_sem.at[i], recv_sem=r_sem.at[1 - i],
            device_id={"rows": g + 1 - 2 * i}, device_id_type=MESH)

    own = [pltpu.make_async_copy(
        p_ref.at[s], ybuf.at[s, pl.ds(pl.multiple_of(me * shard, shard), shard), :],
        local_sem.at[s]) for s in range(sets)]

    barrier = pltpu.get_barrier_semaphore()
    for way in range(2):
        pl.semaphore_signal(barrier, inc=1, device_id={"vec": sides[way]}, device_id_type=MESH)

    @pl.when(has_up)
    def _():
        pl.semaphore_signal(barrier, inc=1, device_id={"rows": g + 1}, device_id_type=MESH)

    @pl.when(has_down)
    def _():
        pl.semaphore_signal(barrier, inc=1, device_id={"rows": g - 1}, device_id_type=MESH)

    for s in range(sets):
        own[s].start()
    edges = max(ng - 1, 1)
    peers = 2 + (edges - g + edges - 1) // edges + (g + edges - 1) // edges
    pl.semaphore_wait(barrier, peers)

    @pl.when(jnp.logical_not(has_up))
    def _():
        grecv[0] = jnp.zeros_like(grecv[0])
        wrecv[0] = jnp.zeros_like(wrecv[0])

    @pl.when(jnp.logical_not(has_down))
    def _():
        grecv[1] = jnp.zeros_like(grecv[1])
        wrecv[1] = jnp.zeros_like(wrecv[1])

    def forward(s, t):
        for way in range(2):
            if t > 0:
                arrived(s, t - 1, way).wait_recv()
            if t < steps:
                sent(s, t, way).start()
        if t == steps:
            own[s].wait()

    order = sorted(((2 * t + 3 * s, s, t) for s in range(sets) for t in range(steps + 1)))
    order = [(0, 0), (1, 0)] + [e[1:] for e in order if e[1:] not in ((0, 0), (1, 0))]

    def run(upto):
        while order:
            event = order.pop(0)
            forward(*event)
            if event == upto:
                return

    def both(src, dst, s_sem, r_sem, act):
        @pl.when(has_up)
        def _():
            act(rim(src, dst, s_sem, r_sem, 0))

        @pl.when(has_down)
        def _():
            act(rim(src, dst, s_sem, r_sem, 1))

    def recv_both(src, dst, s_sem, r_sem):
        @pl.when(has_up)
        def _():
            pltpu.make_async_remote_copy(
                src_ref=src.at[0], dst_ref=dst.at[0], send_sem=s_sem.at[0],
                recv_sem=r_sem.at[0], device_id={"rows": g + 1},
                device_id_type=MESH).wait_recv()

        @pl.when(has_down)
        def _():
            pltpu.make_async_remote_copy(
                src_ref=src.at[1], dst_ref=dst.at[1], send_sem=s_sem.at[1],
                recv_sem=r_sem.at[1], device_id={"rows": g - 1},
                device_id_type=MESH).wait_recv()

    run((0, steps))
    y0 = ybuf[0] + eye_of(2 * width, width)
    y0t = split(y0.T)
    y0 = split(y0)
    gram0 = mm(y0t, y0)
    z = z_ref[...]
    w0 = mm(y0t, split(z))
    run((2, 2) if steps > 2 else (1, steps - 1))
    inv0, = invert_all([gram0])
    if (1, steps) in order:
        run((1, steps))
    ya = ybuf[1, width:, :] + eye_of(width, width)
    yb = ybuf[1, :width, :]
    yat, ybt, ya, yb = split(ya.T), split(yb.T), split(ya), split(yb)
    gram_a = mm(yat, ya)
    gram_b = mm(ybt, yb)
    gsend[0] = gram_a
    gsend[1] = gram_b
    both(gsend, grecv, gs_sem, gr_sem, lambda copy: copy.start())
    run((2, steps - 1))
    z = z - mm(y0, split(mm(split(inv0), split(w0))))
    za, zb = z[width:], z[:width]
    wa = mm(yat, split(za))
    wb = mm(ybt, split(zb))
    wsend[0] = wa
    wsend[1] = wb
    both(wsend, wrecv, ws_sem, wr_sem, lambda copy: copy.start())
    run((2, steps))
    y2 = ybuf[2] + eye_of(2 * width, width)
    y2t = split(y2.T)
    y2 = split(y2)
    gram2 = mm(y2t, y2)
    recv_both(gsend, grecv, gs_sem, gr_sem)
    inv_a, inv_b, inv2 = invert_all([gram_a + grecv[0], gram_b + grecv[1], gram2])
    recv_both(wsend, wrecv, ws_sem, wr_sem)
    xa = split(mm(split(inv_a), split(wa + wrecv[0])))
    xb = split(mm(split(inv_b), split(wb + wrecv[1])))
    za = jnp.where(has_up, za - mm(ya, xa), za)
    zb = jnp.where(has_down, zb - mm(yb, xb), zb)
    z = jnp.concatenate([zb, za], axis=0)
    x2 = mm(split(inv2), split(mm(y2t, split(z))))
    out_ref[...] = z - mm(y2, split(x2))

    for s in range(sets):
        for way in range(2):
            for t in range(steps):
                sent(s, t, way).wait_send()
    both(gsend, grecv, gs_sem, gr_sem, lambda copy: copy.wait_send())
    both(wsend, wrecv, ws_sem, wr_sem, lambda copy: copy.wait_send())


def local(n, ng, eigen_rows, panels):
    sets, shard, width = panels.shape
    rows, columns = eigen_rows.shape
    dma = pltpu.SemaphoreType.DMA
    return pl.pallas_call(
        functools.partial(kernel, n, ng),
        out_shape=jax.ShapeDtypeStruct(eigen_rows.shape, F32),
        in_specs=[pl.BlockSpec(memory_space=pltpu.VMEM), pl.BlockSpec(memory_space=pl.ANY)],
        out_specs=pl.BlockSpec(memory_space=pltpu.VMEM),
        scratch_shapes=[
            pltpu.VMEM((sets, n * shard, width), F32),
            pltpu.VMEM((2, width, width), F32),
            pltpu.VMEM((2, width, width), F32),
            pltpu.VMEM((2, width, columns), F32),
            pltpu.VMEM((2, width, columns), F32),
            dma((sets,)),
            dma((sets, 2, n // 2)),
            dma((sets, 2, n // 2)),
            dma((2,)), dma((2,)), dma((2,)), dma((2,)),
        ],
        compiler_params=pltpu.CompilerParams(
            collective_id=0, has_side_effects=True, vmem_limit_bytes=48 * 2**20
        ),
        name="sweeps",
    )(eigen_rows, panels)


def solution(mesh):
    in_specs = (P("rows", "vec"), P(None, ("rows", "vec"), None))
    return jax.shard_map(
        functools.partial(local, mesh.shape["vec"], mesh.shape["rows"]),
        mesh=mesh, in_specs=in_specs, out_specs=P("rows", "vec"), check_vma=False)
```

```python
import functools

import jax
import jax.numpy as jnp
from jax import lax
from jax.experimental import pallas as pl
from jax.experimental.pallas import tpu as pltpu
from jax.sharding import PartitionSpec as P

MESH = pl.DeviceIdType.MESH
BASE = 8
F32, BF16 = jnp.float32, jnp.bfloat16


def split(a):
    high = a.astype(BF16)
    return high, (a - high.astype(F32)).astype(BF16)


def mm(a, b):
    ah, al = a
    bh, bl = b
    n = bh.shape[1]
    if n % 256:
        both = jnp.concatenate([bh, bl], axis=1)
        left = jnp.concatenate([ah, al], axis=1)
        out = jnp.dot(
            left, jnp.concatenate([both, both], axis=0), preferred_element_type=F32
        )
        return out[:, :n] + out[:, n:]
    dot = functools.partial(jnp.dot, preferred_element_type=F32)
    return dot(ah, bh) + (dot(ah, bl) + dot(al, bh))


def eye_of(rows, cols):
    r = lax.broadcasted_iota(jnp.int32, (rows, cols), 0)
    c = lax.broadcasted_iota(jnp.int32, (rows, cols), 1)
    return jnp.where(r == c, 1.0, 0.0).astype(F32)


def upper(gram):
    half = gram.shape[0] // 2
    return jnp.concatenate(
        [gram[:half, :half], gram[:half, half:], gram[half:, half:]], axis=0)


def invert_all(grams):
    half = grams[0].shape[1]
    r = lax.broadcasted_iota(jnp.int32, (half, half), 0)
    c = lax.broadcasted_iota(jnp.int32, (half, half), 1)
    eye = jnp.where(r == c, 1.0, 0.0).astype(F32)
    parts, corners, scales = [], [], []
    for g in grams:
        d_rows = []
        d_cols = []
        for i in range(2):
            tile = g[2 * i * half : (2 * i + 1) * half]
            diag = jnp.where(r == c, 0.5 * tile, 0.0)
            d_rows.append(1.0 / jnp.sum(diag, axis=0, keepdims=True))
            d_cols.append(1.0 / jnp.sum(diag, axis=1, keepdims=True))
            parts.append(jnp.where(c > r, tile * d_rows[i], 0.0))
        corners.append(g[half : 2 * half] * d_rows[1])
        scales.append(d_cols)
    small = [jnp.where(r // BASE == c // BASE, m, 0.0) for m in parts]
    pairs = [split(m) for m in small]
    powers = [mm(p, p) for p in pairs]
    inv = [eye - m for m in small]
    span = 2
    while span < BASE:
        pairs = [split(p) for p in powers]
        inv = [i + mm(split(i), p) for i, p in zip(inv, pairs)]
        span *= 2
        if span < BASE:
            powers = [mm(p, p) for p in pairs]
        else:
            break
    span = BASE
    while span < half:
        mask = jnp.logical_and(r // (2 * span) == c // (2 * span), r // span != c // span)
        cross = [split(jnp.where(mask, m, 0.0)) for m in parts]
        pairs = [split(i) for i in inv]
        mid = [mm(x, p) for x, p in zip(cross, pairs)]
        inv = [i - mm(p, split(m)) for i, p, m in zip(inv, pairs, mid)]
        span *= 2
    pairs = [split(i) for i in inv]
    mids = [mm(split(corners[k]), pairs[2 * k + 1]) for k in range(len(grams))]
    tops = [-mm(pairs[2 * k], split(mids[k])) for k in range(len(grams))]
    out = []
    for k in range(len(grams)):
        upper = jnp.concatenate([inv[2 * k], tops[k]], axis=1) * scales[k][0]
        lower = jnp.concatenate([jnp.zeros_like(tops[k]), inv[2 * k + 1]], axis=1) * scales[k][1]
        out.append(jnp.concatenate([upper, lower], axis=0))
    return out


def kernel(n, ng, z_ref, p_ref, out_ref, zbuf, z_sem, ybuf, gsend, grecv, wsend, wrecv,
           local_sem, send_sem, recv_sem, gs_sem, gr_sem, ws_sem, wr_sem):
    sets, shard, width = p_ref.shape
    steps = n // 2
    hw = width // 2
    g = lax.axis_index("rows")
    me = lax.axis_index("vec")
    odd = me % 2
    pos = (1 - odd) * (me // 2) + odd * (n - 1 - me // 2)

    def index_of(q):
        q = (q + 2 * n) % n
        first = 1 - (2 * q) // n
        return first * (2 * q) + (1 - first) * (2 * (n - 1 - q) + 1)

    sides = (index_of(pos + 1), index_of(pos - 1))
    has_up = g < ng - 1
    has_down = g > 0

    def slot(s, q, t, way):
        rows = pl.ds(pl.multiple_of(index_of(q) * shard, shard), shard)
        if t < steps - 1:
            return ybuf.at[s, rows, :]
        return ybuf.at[s, rows, pl.ds(way * hw, hw)]

    def sent(s, t, way):
        sign = 1 - 2 * way
        ref = slot(s, pos - sign * t, t, way)
        src = p_ref.at[s] if t == 0 and steps > 1 else ref
        return pltpu.make_async_remote_copy(
            src_ref=src, dst_ref=ref,
            send_sem=send_sem.at[s, way, t], recv_sem=recv_sem.at[s, way, t],
            device_id={"vec": sides[way]}, device_id_type=MESH)

    def arrived(s, t, way):
        sign = 1 - 2 * way
        ref = slot(s, pos - sign * (t + 1), t, way)
        return pltpu.make_async_remote_copy(
            src_ref=ref, dst_ref=ref,
            send_sem=send_sem.at[s, way, t], recv_sem=recv_sem.at[s, way, t],
            device_id={"vec": sides[way]}, device_id_type=MESH)

    def rim(src, dst, s_sem, r_sem, i):
        return pltpu.make_async_remote_copy(
            src_ref=src.at[i], dst_ref=dst.at[1 - i],
            send_sem=s_sem.at[i], recv_sem=r_sem.at[1 - i],
            device_id={"rows": g + 1 - 2 * i}, device_id_type=MESH)

    own = [pltpu.make_async_copy(
        p_ref.at[s], ybuf.at[s, pl.ds(pl.multiple_of(me * shard, shard), shard), :],
        local_sem.at[s]) for s in range(sets)]

    barrier = pltpu.get_barrier_semaphore()
    for way in range(2):
        pl.semaphore_signal(barrier, inc=1, device_id={"vec": sides[way]}, device_id_type=MESH)

    @pl.when(has_up)
    def _():
        pl.semaphore_signal(barrier, inc=1, device_id={"rows": g + 1}, device_id_type=MESH)

    @pl.when(has_down)
    def _():
        pl.semaphore_signal(barrier, inc=1, device_id={"rows": g - 1}, device_id_type=MESH)

    for s in range(sets):
        own[s].start()
    z_copy = pltpu.make_async_copy(z_ref, zbuf, z_sem)
    z_copy.start()
    edges = max(ng - 1, 1)
    peers = 2 + (edges - g + edges - 1) // edges + (g + edges - 1) // edges
    pl.semaphore_wait(barrier, peers)

    @pl.when(jnp.logical_not(has_up))
    def _():
        grecv[0] = jnp.zeros_like(grecv[0])
        wrecv[0] = jnp.zeros_like(wrecv[0])

    @pl.when(jnp.logical_not(has_down))
    def _():
        grecv[1] = jnp.zeros_like(grecv[1])
        wrecv[1] = jnp.zeros_like(wrecv[1])

    def forward(s, t):
        for way in range(2):
            if t > 0:
                arrived(s, t - 1, way).wait_recv()
            if t < steps:
                sent(s, t, way).start()
        if t == steps:
            own[s].wait()

    ranks = {1: 0, 0: 1, 2: 2}
    order = sorted((2 * t + ranks[s] if t else 0, ranks[s], s, t)
                   for s in range(sets) for t in range(steps + 1))
    order = [e[2:] for e in order]

    def run(upto):
        while order:
            event = order.pop(0)
            forward(*event)
            if event == upto:
                return

    def both(src, dst, s_sem, r_sem, act):
        @pl.when(has_up)
        def _():
            act(rim(src, dst, s_sem, r_sem, 0))

        @pl.when(has_down)
        def _():
            act(rim(src, dst, s_sem, r_sem, 1))

    def recv_both(src, dst, s_sem, r_sem):
        @pl.when(has_up)
        def _():
            pltpu.make_async_remote_copy(
                src_ref=src.at[0], dst_ref=dst.at[0], send_sem=s_sem.at[0],
                recv_sem=r_sem.at[0], device_id={"rows": g + 1},
                device_id_type=MESH).wait_recv()

        @pl.when(has_down)
        def _():
            pltpu.make_async_remote_copy(
                src_ref=src.at[1], dst_ref=dst.at[1], send_sem=s_sem.at[1],
                recv_sem=r_sem.at[1], device_id={"rows": g - 1},
                device_id_type=MESH).wait_recv()

    run((1, steps))
    run((2, steps - 1))
    ya = ybuf[1, width:, :] + eye_of(width, width)
    yb = ybuf[1, :width, :]
    yat, ybt, ya, yb = split(ya.T), split(yb.T), split(ya), split(yb)
    gram_a = upper(mm(yat, ya))
    gram_b = upper(mm(ybt, yb))
    gsend[0] = gram_a
    gsend[1] = gram_b
    both(gsend, grecv, gs_sem, gr_sem, lambda copy: copy.start())
    z_copy.wait()
    z = zbuf[...]
    run((0, steps))
    y0 = ybuf[0] + eye_of(2 * width, width)
    y0t = split(y0.T)
    y0 = split(y0)
    w0 = mm(y0t, split(z))
    inv0, = invert_all([upper(mm(y0t, y0))])
    z = z - mm(y0, split(mm(split(inv0), split(w0))))
    za, zb = z[width:], z[:width]
    wa = mm(yat, split(za))
    wb = mm(ybt, split(zb))
    wsend[0] = wa
    wsend[1] = wb
    both(wsend, wrecv, ws_sem, wr_sem, lambda copy: copy.start())
    run((2, steps))
    y2 = ybuf[2] + eye_of(2 * width, width)
    y2t = split(y2.T)
    y2 = split(y2)
    gram2 = upper(mm(y2t, y2))
    recv_both(gsend, grecv, gs_sem, gr_sem)
    inv_a, inv_b, inv2 = invert_all([gram_a + grecv[0], gram_b + grecv[1], gram2])
    recv_both(wsend, wrecv, ws_sem, wr_sem)
    xa = split(mm(split(inv_a), split(wa + wrecv[0])))
    xb = split(mm(split(inv_b), split(wb + wrecv[1])))
    za = jnp.where(has_up, za - mm(ya, xa), za)
    zb = jnp.where(has_down, zb - mm(yb, xb), zb)
    z = jnp.concatenate([zb, za], axis=0)
    x2 = mm(split(inv2), split(mm(y2t, split(z))))
    out_ref[...] = z - mm(y2, split(x2))

    for s in range(sets):
        for way in range(2):
            for t in range(steps):
                sent(s, t, way).wait_send()
    both(gsend, grecv, gs_sem, gr_sem, lambda copy: copy.wait_send())
    both(wsend, wrecv, ws_sem, wr_sem, lambda copy: copy.wait_send())


def local(n, ng, eigen_rows, panels):
    sets, shard, width = panels.shape
    rows, columns = eigen_rows.shape
    dma = pltpu.SemaphoreType.DMA
    return pl.pallas_call(
        functools.partial(kernel, n, ng),
        out_shape=jax.ShapeDtypeStruct(eigen_rows.shape, F32),
        in_specs=[pl.BlockSpec(memory_space=pl.ANY)] * 2,
        out_specs=pl.BlockSpec(memory_space=pltpu.VMEM),
        scratch_shapes=[
            pltpu.VMEM((rows, columns), F32),
            dma(()),
            pltpu.VMEM((sets, n * shard, width), F32),
            pltpu.VMEM((2, width // 2 * 3, width // 2), F32),
            pltpu.VMEM((2, width // 2 * 3, width // 2), F32),
            pltpu.VMEM((2, width, columns), F32),
            pltpu.VMEM((2, width, columns), F32),
            dma((sets,)),
            dma((sets, 2, n // 2)),
            dma((sets, 2, n // 2)),
            dma((2,)), dma((2,)), dma((2,)), dma((2,)),
        ],
        compiler_params=pltpu.CompilerParams(
            collective_id=0, has_side_effects=True, vmem_limit_bytes=48 * 2**20
        ),
        name="sweeps",
    )(eigen_rows, panels)


def solution(mesh):
    in_specs = (P("rows", "vec"), P(None, ("rows", "vec"), None))
    return jax.shard_map(
        functools.partial(local, mesh.shape["vec"], mesh.shape["rows"]),
        mesh=mesh, in_specs=in_specs, out_specs=P("rows", "vec"), check_vma=False)
```
